32 devices in a mesh: dp: 8 (over y, x, core), tensor: 4 (over z).
Axes of the slice: x: 2, y: 2, z: 4, core: 2. Of those that a mesh axis runs over, the one named last changes fastest.
Arguments:
- images: bfloat16 [32, 577, 1024], P('dp'), may hold values from -6 to 6
- first_gain: float32 [1024], replicated, may hold values from 0.5 to 1.5
- first_shift: float32 [1024], replicated, may hold values from -1 to 1
- qkv_weight: bfloat16 [1024, 3, 1024], P(None, None, 'tensor'), may hold values from -0.1875 to 0.1875
- query_bias: float32 [1024], P('tensor'), may hold values from -2.5 to 2.5
- value_bias: float32 [1024], P('tensor'), may hold values from -2.5 to 2.5
- output_weight: bfloat16 [1024, 1024], P('tensor'), may hold values from -2 to 2
- output_bias: float32 [1024], replicated, may hold values from -2.5 to 2.5
- second_gain: float32 [1024], replicated, may hold values from 0.5 to 1.5
- second_shift: float32 [1024], replicated, may hold values from -1 to 1
- expand_weight: bfloat16 [1024, 4096], P(None, 'tensor'), may hold values from -0.1875 to 0.1875
- expand_bias: float32 [4096], P('tensor'), may hold values from -2.5 to 2.5
- shrink_weight: bfloat16 [4096, 1024], P('tensor'), may hold values from -0.125 to 0.125
- shrink_bias: float32 [1024], replicated, may hold values from -2.5 to 2.5
- cotangent: bfloat16 [32, 577, 1024], P('dp'), may hold values from -6 to 6
Outputs:
- result: bfloat16 [32, 577, 1024], P('dp')
- grad_images: float32 [32, 577, 1024], P('dp')
- grad_first_gain: float32 [1024], replicated
- grad_first_shift: float32 [1024], replicated
- grad_qkv_weight: float32 [1024, 3, 1024], P(None, None, 'tensor')
- grad_query_bias: float32 [1024], P('tensor')
- grad_value_bias: float32 [1024], P('tensor')
- grad_output_weight: float32 [1024, 1024], P('tensor')
- grad_output_bias: float32 [1024], replicated
- grad_second_gain: float32 [1024], replicated
- grad_second_shift: float32 [1024], replicated
- grad_expand_weight: float32 [1024, 4096], P(None, 'tensor')
- grad_expand_bias: float32 [4096], P('tensor')
- grad_shrink_weight: float32 [4096, 1024], P('tensor')
- grad_shrink_bias: float32 [1024], replicated
The draws below stay inside these ranges and needn't reach their ends.
All inputs are finite; a program needn't handle non-finite values.
Results may differ from the reference program's by a relative error of at most 0.018.
Values may be sent and summed in bfloat16 or wider, within the bound.
A program may use at most 192 MiB of HBM per device.

```python
import jax
import jax.numpy as jnp
from jax import lax

D = 1024
HEADS = 16
HEAD_DIM = 64
FF = 4096
SEQ_LEN = 577
IMG_DEV = 4
IMAGES = 32
N_TENSOR = 4


def level_of(rng, dims, shards, least, top_value):
    level, own = 1.0, jax.random.fold_in(rng, 6)
    for axis_at, blocks in shards:
        draws = jnp.exp(jax.random.uniform(jax.random.fold_in(own, axis_at), (blocks,), jnp.float32, least / len(shards), top_value / len(shards)))
        level = level * jnp.repeat(draws, dims[axis_at] // blocks).reshape([-1 if axis == axis_at else 1 for axis in range(len(dims))])
    return level


def scatter_about(key, dims, scale, most, shards=(), kind=jnp.bfloat16):
    array = scale * jax.random.normal(key, dims, jnp.float32)
    if shards:
        array = array * level_of(key, dims, shards, -0.22, 0.18)
    return jnp.clip(array, -most, most).astype(kind)


def setup_inputs(seed: int = 0) -> dict:
    key_of = jax.random.split(jax.random.key(seed), 16)
    images = scatter_about(key_of[0], (IMAGES, SEQ_LEN, D), 1.0, 6.0, ((0, 8),))
    first_gain = jnp.clip(1.0 + 0.1 * jax.random.normal(key_of[1], (D,), jnp.float32), 0.5, 1.5)
    first_shift = scatter_about(key_of[2], (D,), 0.2, 1.0, (), jnp.float32)
    qkv_weight = scatter_about(key_of[3], (D, 3, D), D ** -0.5, 0.1875, ((2, 4),))
    query_bias = scatter_about(key_of[4], (D,), 0.5, 2.5, ((0, 4),), jnp.float32)
    value_bias = scatter_about(key_of[5], (D,), 0.5, 2.5, ((0, 4),), jnp.float32)
    output_weight = scatter_about(key_of[6], (D, D), (D // 128) ** -0.5, 2.0, ((0, 4),))
    output_bias = scatter_about(key_of[7], (D,), 0.5, 2.5, (), jnp.float32)
    second_gain = jnp.clip(1.0 + 0.1 * jax.random.normal(key_of[8], (D,), jnp.float32), 0.5, 1.5)
    second_shift = scatter_about(key_of[9], (D,), 0.2, 1.0, (), jnp.float32)
    expand_weight = scatter_about(key_of[10], (D, FF), D ** -0.5, 0.1875, ((1, 4),))
    expand_bias = scatter_about(key_of[11], (FF,), 0.5, 2.5, ((0, 4),), jnp.float32)
    shrink_weight = scatter_about(key_of[12], (FF, D), (FF // 2) ** -0.5, 0.125, ((0, 4),))
    shrink_bias = scatter_about(key_of[13], (D,), 0.5, 2.5, (), jnp.float32)
    cotangent = scatter_about(key_of[14], (IMAGES, SEQ_LEN, D), 1.0, 6.0, ((0, 8),))
    return {"images": images, "first_gain": first_gain, "first_shift": first_shift, "qkv_weight": qkv_weight, "query_bias": query_bias, "value_bias": value_bias, "output_weight": output_weight, "output_bias": output_bias, "second_gain": second_gain, "second_shift": second_shift, "expand_weight": expand_weight, "expand_bias": expand_bias, "shrink_weight": shrink_weight, "shrink_bias": shrink_bias, "cotangent": cotangent}


@jax.custom_vjp
def low(v):
    return lax.optimization_barrier(v.astype(jnp.bfloat16)).astype(jnp.float32)

@jax.custom_vjp
def low_back(v):
    return v

def low_keep(v):
    return (low(v), None)

def low_pass(kept, grad):
    return (grad,)

def back_keep(v):
    return (v, None)

def back_low(kept, grad):
    return (low(grad),)
low.defvjp(low_keep, low_pass)
low_back.defvjp(back_keep, back_low)
HIGH = lax.Precision.HIGHEST

def layer_norm(value, gain, shift):
    centre = lax.optimization_barrier(jnp.mean(value, -1, keepdims=True))
    spread = lax.optimization_barrier(jnp.mean((value - centre) * (value - centre), -1, keepdims=True))
    return (value - centre) * lax.rsqrt(spread + 1e-06) * gain + shift

def attend(block):
    query, keys, values = block
    scores = low_back(jnp.einsum('shd,thd->hst', query, keys, precision=HIGH) * HEAD_DIM ** (-0.5))
    probs = low(jax.nn.softmax(scores, -1))
    return jnp.einsum('hst,thd->shd', probs, values, precision=HIGH)

def forward(images, params):
    first_gain, first_shift, qkv_weight, query_bias, value_bias, output_weight, output_bias, second_gain, second_shift, expand_weight, expand_bias, shrink_weight, shrink_bias = params
    groups = N_TENSOR
    local = D // groups
    hidden = FF // groups
    count = images.shape[0]
    tokens = images.reshape(-1, D)
    rows = tokens.shape[0]
    normed = low(layer_norm(tokens, first_gain, first_shift))
    copies = low_back(jnp.broadcast_to(normed, (groups, rows, D)))
    weight = qkv_weight.reshape(D, 3, groups, local)
    packed = jnp.einsum('gnd,djgc->gnjc', copies, weight, precision=HIGH)
    biases = jnp.stack([query_bias, jnp.zeros_like(query_bias), value_bias]).reshape(3, groups, local)
    packed = packed + jnp.transpose(biases, (1, 0, 2))[:, None]
    packed = low_back(low(packed))
    packed = jnp.transpose(packed, (1, 2, 0, 3)).reshape(count, SEQ_LEN, 3, HEADS, HEAD_DIM)
    mixed = lax.map(jax.checkpoint(attend), (packed[:, :, 0], packed[:, :, 1], packed[:, :, 2]))
    mixed = low_back(low(mixed)).reshape(rows, groups, local)
    mixed = jnp.transpose(mixed, (1, 0, 2))
    parts = low(jnp.einsum('gnc,gcd->gnd', mixed, output_weight.reshape(groups, local, D), precision=HIGH))
    middle = tokens + low_back(lax.optimization_barrier(jnp.sum(parts, 0))) + output_bias
    normed_two = low(layer_norm(middle, second_gain, second_shift))
    copies_two = low_back(jnp.broadcast_to(normed_two, (groups, rows, D)))
    before = jnp.einsum('gnd,dgf->gnf', copies_two, expand_weight.reshape(D, groups, hidden), precision=HIGH)
    before = low_back(before + expand_bias.reshape(groups, 1, hidden))
    active = low(jax.nn.gelu(before, approximate=False))
    parts_two = low(jnp.einsum('gnf,gfd->gnd', active, shrink_weight.reshape(groups, hidden, D), precision=HIGH))
    output = middle + low_back(lax.optimization_barrier(jnp.sum(parts_two, 0))) + shrink_bias
    return output.reshape(count, SEQ_LEN, D)

def reference(images, first_gain, first_shift, qkv_weight, query_bias, value_bias, output_weight, output_bias, second_gain, second_shift, expand_weight, expand_bias, shrink_weight, shrink_bias, cotangent):
    params = tuple((p.astype(jnp.float32) for p in (first_gain, first_shift, qkv_weight, query_bias, value_bias, output_weight, output_bias, second_gain, second_shift, expand_weight, expand_bias, shrink_weight, shrink_bias)))
    batches = IMAGES // IMG_DEV
    inputs = images.astype(jnp.float32).reshape(batches, IMG_DEV, SEQ_LEN, D)
    grads_in = cotangent.astype(jnp.float32).reshape(batches, IMG_DEV, SEQ_LEN, D)

    def stepper(totals, pair):
        block, grad_block = pair
        output, pull = jax.vjp(forward, block, params)
        grad_input, grad_params = pull(grad_block)
        totals = jax.tree.map(lambda a, b: a + b, totals, grad_params)
        return (totals, (output, grad_input))
    zeros = jax.tree.map(jnp.zeros_like, params)
    totals, (outputs, grad_inputs) = lax.scan(stepper, zeros, (inputs, grads_in))
    result = outputs.reshape(IMAGES, SEQ_LEN, D).astype(jnp.bfloat16)
    grad_images = grad_inputs.reshape(IMAGES, SEQ_LEN, D)
    return (result, grad_images) + tuple(totals)
```

```python
import functools

import jax
import jax.numpy as jnp
from jax import lax
from jax.experimental import pallas as pl
from jax.experimental.pallas import tpu as pltpu
from jax.sharding import PartitionSpec as P

HEAD_DIM = 64
BF = jnp.bfloat16
F32 = jnp.float32


def dot(a, b, ca, cb):
    return lax.dot_general(a, b, (((ca,), (cb,)), ((), ())), preferred_element_type=F32)


def layer_norm(value, gain, shift):
    centre = jnp.mean(value, -1, keepdims=True)
    centred = value - centre
    inverse = lax.rsqrt(jnp.mean(centred * centred, -1, keepdims=True) + 1e-06)
    normed = centred * inverse
    return (normed * gain + shift, normed, inverse)


def norm_back(upstream, normed, inverse, gain):
    scaled = upstream * gain
    return inverse * (
        scaled
        - jnp.mean(scaled, -1, keepdims=True)
        - normed * jnp.mean(scaled * normed, -1, keepdims=True)
    )


def attend_kernel(packed_ref, out_ref):
    local = out_ref.shape[-1]
    factor = HEAD_DIM ** (-0.5)
    for head in range(local // HEAD_DIM):
        at = head * HEAD_DIM
        query = packed_ref[:, at : at + HEAD_DIM] * jnp.asarray(factor, BF)
        key = packed_ref[:, local + at : local + at + HEAD_DIM]
        value = packed_ref[:, 2 * local + at : 2 * local + at + HEAD_DIM]
        scores = dot(query, key, 1, 1)
        expanded = jnp.exp(scores - jnp.max(scores, -1, keepdims=True))
        probs = expanded * (1.0 / jnp.sum(expanded, -1, keepdims=True))
        out_ref[:, at : at + HEAD_DIM] = dot(probs.astype(BF), value, 1, 0).astype(BF)


def attend_back_kernel(packed_ref, grad_ref, out_ref):
    local = grad_ref.shape[-1]
    factor = HEAD_DIM ** (-0.5)
    for head in range(local // HEAD_DIM):
        at = head * HEAD_DIM
        query = packed_ref[:, at : at + HEAD_DIM] * jnp.asarray(factor, BF)
        key = packed_ref[:, local + at : local + at + HEAD_DIM]
        value = packed_ref[:, 2 * local + at : 2 * local + at + HEAD_DIM]
        grad = grad_ref[:, at : at + HEAD_DIM]
        scores = dot(key, query, 1, 1)
        expanded = jnp.exp(scores - jnp.max(scores, 0, keepdims=True))
        probs = expanded * (1.0 / jnp.sum(expanded, 0, keepdims=True))
        grad_probs = dot(value, grad, 1, 1)
        inner = jnp.sum(grad_probs * probs, 0, keepdims=True)
        grad_scores = (probs * (grad_probs - inner)).astype(BF)
        out_ref[:, at : at + HEAD_DIM] = (dot(grad_scores, key, 0, 0) * factor).astype(BF)
        out_ref[:, local + at : local + at + HEAD_DIM] = dot(grad_scores, query, 1, 0).astype(BF)
        out_ref[:, 2 * local + at : 2 * local + at + HEAD_DIM] = dot(
            probs.astype(BF), grad, 1, 0
        ).astype(BF)


def attention(packed, groups):
    count, length, width = packed.shape
    block = width // groups
    local = block // 3
    heads = count * groups * local // HEAD_DIM
    return pl.pallas_call(
        attend_kernel,
        grid=(count, groups),
        in_specs=[pl.BlockSpec((None, length, block), lambda i, g: (i, 0, g))],
        out_specs=pl.BlockSpec((None, length, local), lambda i, g: (i, 0, g)),
        out_shape=jax.ShapeDtypeStruct((count, length, width // 3), BF),
        compiler_params=pltpu.CompilerParams(vmem_limit_bytes=40 * 2**20),
        cost_estimate=pl.CostEstimate(
            flops=heads * 4 * length * length * HEAD_DIM * 8,
            bytes_accessed=count * length * width * 3,
            transcendentals=heads * length * length,
        ),
        name="attend",
    )(packed)


def attention_back(packed, grad, groups):
    count, length, width = packed.shape
    block = width // groups
    local = block // 3
    heads = count * groups * local // HEAD_DIM
    return pl.pallas_call(
        attend_back_kernel,
        grid=(count, groups),
        in_specs=[
            pl.BlockSpec((None, length, block), lambda i, g: (i, 0, g)),
            pl.BlockSpec((None, length, local), lambda i, g: (i, 0, g)),
        ],
        out_specs=pl.BlockSpec((None, length, block), lambda i, g: (i, 0, g)),
        out_shape=jax.ShapeDtypeStruct((count, length, width), BF),
        compiler_params=pltpu.CompilerParams(vmem_limit_bytes=40 * 2**20),
        cost_estimate=pl.CostEstimate(
            flops=heads * 10 * length * length * HEAD_DIM * 8,
            bytes_accessed=count * length * width * 5,
            transcendentals=heads * length * length,
        ),
        name="attend_back",
    )(packed, grad)


def shards(
    groups,
    images,
    first_gain,
    first_shift,
    qkv_weight,
    query_bias,
    value_bias,
    output_weight,
    output_bias,
    second_gain,
    second_shift,
    expand_weight,
    expand_bias,
    shrink_weight,
    shrink_bias,
    cotangent,
):
    total_count, length, width = images.shape
    ways = lax.axis_size("dp")
    rank, group = lax.axis_index("dp"), lax.axis_index("tensor")
    count = total_count // groups
    local = qkv_weight.shape[2]
    hidden = expand_weight.shape[1]
    rows = count * length
    part = width // ways

    def shifted(value, step):
        return lax.ppermute(value, "tensor", [(i, (i + step) % groups) for i in range(groups)])

    def source(step):
        return lax.rem(group + groups - step, groups)

    def gather_tensor(value, axis, kind):
        size = value.shape[axis]
        shape = list(value.shape)
        shape[axis] = size * groups
        whole = jnp.zeros(shape, kind)
        for step in range(groups):
            piece = shifted(value, step) if step else value
            whole = lax.dynamic_update_slice_in_dim(
                whole, piece.astype(kind), source(step) * size, axis
            )
        return whole

    def spread(piece):
        return lax.all_gather(gather_tensor(piece, 1, BF), "dp", axis=0, tiled=True)

    def scatter_tensor(parts):
        def toward(step):
            to = lax.rem(group + step, groups)
            taken = []
            for array in parts:
                size = array.shape[1] // groups
                taken.append(lax.dynamic_slice_in_dim(array, to * size, size, 1))
            return jnp.concatenate(taken, 1) if len(taken) > 1 else taken[0]

        total = toward(0).astype(F32)
        for step in range(1, groups):
            total = total + shifted(toward(step), step).astype(F32)
        return total.astype(BF)

    def scatter_rows(grad):
        return lax.psum_scatter(grad, "dp", scatter_dimension=0, tiled=True)

    start = rank * part
    qkv_piece = lax.dynamic_slice_in_dim(qkv_weight, start, part, 0)
    qkv_piece = jnp.concatenate([qkv_piece[:, 0], qkv_piece[:, 1], qkv_piece[:, 2]], 1)
    output_piece = lax.dynamic_slice_in_dim(output_weight, start, part, 1).T
    expand_piece = lax.dynamic_slice_in_dim(expand_weight, start, part, 0)
    shrink_piece = lax.dynamic_slice_in_dim(shrink_weight, start, part, 1).T
    biases = jnp.concatenate([query_bias, value_bias, expand_bias])[None]
    biases = gather_tensor(biases, 0, F32)
    qkv_full = spread(qkv_piece)
    output_full = spread(output_piece)
    expand_full = spread(expand_piece)
    shrink_full = spread(shrink_piece)
    expand_bias_full = biases[:, 2 * local :].reshape(-1)
    qkv_bias_full = jnp.concatenate(
        [biases[:, :local], jnp.zeros((groups, local), F32), biases[:, local : 2 * local]], 1
    ).reshape(-1)

    tokens = lax.dynamic_slice_in_dim(images, group * count, count, 0)
    tokens = tokens.reshape(rows, width).astype(F32)
    upstream = lax.dynamic_slice_in_dim(cotangent, group * count, count, 0).reshape(rows, width)
    up_float = upstream.astype(F32)
    first_out, first_normed, first_inverse = layer_norm(tokens, first_gain, first_shift)
    first_low = first_out.astype(BF)
    packed = (dot(first_low, qkv_full, 1, 0) + qkv_bias_full).astype(BF)
    packed = packed.reshape(count, length, 3 * width)
    mixed = attention(packed, groups).reshape(rows, width)
    middle = tokens + dot(mixed, output_full, 1, 1) + output_bias
    second_out, second_normed, second_inverse = layer_norm(middle, second_gain, second_shift)
    second_low = second_out.astype(BF)
    before = dot(second_low, expand_full, 1, 0) + expand_bias_full
    lower = 0.5 + 0.5 * lax.erf(before * (0.5**0.5))
    active = (before * lower).astype(BF)
    slope = lower + before * (jnp.exp(-0.5 * before * before) * 0.3989422804014327)
    active, slope = lax.optimization_barrier((active, slope))
    output = middle + dot(active, shrink_full, 1, 1) + shrink_bias
    result = output.astype(BF).reshape(count, length, width)
    result = gather_tensor(result, 0, BF)

    shrink_grad = dot(upstream, active, 0, 0).astype(BF)
    upstream, shrink_grad = lax.optimization_barrier((upstream, shrink_grad))
    shrink_grad = scatter_rows(shrink_grad)
    grad_before = (dot(upstream, shrink_full, 1, 0) * slope).astype(BF)
    expand_grad = dot(second_low, grad_before, 0, 0).astype(BF)
    grad_before, expand_grad = lax.optimization_barrier((grad_before, expand_grad))
    expand_grad = scatter_rows(expand_grad)
    grad_second_out = dot(grad_before, expand_full, 1, 1)
    grad_middle = up_float + norm_back(grad_second_out, second_normed, second_inverse, second_gain)
    grad_attn_low = grad_middle.astype(BF)
    output_grad = dot(grad_attn_low, mixed, 0, 0).astype(BF)
    grad_mixed = dot(grad_attn_low, output_full, 1, 0).astype(BF).reshape(count, length, width)
    grad_packed = attention_back(packed, grad_mixed, groups).reshape(rows, 3 * width)
    qkv_grad = dot(first_low, grad_packed, 0, 0).astype(BF)
    attn_grad = scatter_rows(jnp.concatenate([qkv_grad, output_grad], 1))
    attn_grad = scatter_tensor([attn_grad[:, : 3 * width], attn_grad[:, 3 * width :]])
    mlp_grad = scatter_tensor([expand_grad, shrink_grad])
    mlp_grad = lax.all_gather(mlp_grad, "dp", axis=0, tiled=True)
    attn_grad = lax.all_gather(attn_grad, "dp", axis=0, tiled=True)
    qkv_grad, output_grad = attn_grad[:, : 3 * local], attn_grad[:, 3 * local :]
    expand_grad, shrink_grad = mlp_grad[:, :hidden], mlp_grad[:, hidden:]
    grad_first_out = dot(grad_packed, qkv_full, 1, 1)
    grad_images = grad_middle + norm_back(grad_first_out, first_normed, first_inverse, first_gain)
    grad_images = grad_images.astype(BF).reshape(count, length, width)
    grad_images = lax.optimization_barrier(grad_images)
    grad_images = gather_tensor(grad_images, 0, F32)

    packed_bias = jnp.sum(grad_packed.astype(F32), 0).reshape(groups, 3, local)
    vectors = [
        jnp.sum(grad_first_out * first_normed, 0),
        jnp.sum(grad_first_out, 0),
        packed_bias[:, 0].reshape(-1),
        packed_bias[:, 2].reshape(-1),
        jnp.sum(grad_middle, 0),
        jnp.sum(grad_second_out * second_normed, 0),
        jnp.sum(grad_second_out, 0),
        jnp.sum(grad_before.astype(F32), 0),
        jnp.sum(up_float, 0),
    ]
    sizes = [v.shape[0] for v in vectors]
    summed = jnp.sum(gather_tensor(jnp.concatenate(vectors)[None], 0, F32), 0)
    summed = lax.psum(summed, "dp")
    pieces, at = [], 0
    for size in sizes:
        pieces.append(lax.slice_in_dim(summed, at, at + size))
        at += size
    first_gain_g, first_shift_g, query_g, value_g, output_g = pieces[:5]
    second_gain_g, second_shift_g, expand_g, shrink_g = pieces[5:]

    def own(vector, size):
        return lax.dynamic_slice_in_dim(vector, group * size, size, 0)

    qkv_grad = jnp.stack(
        [qkv_grad[:, :local], qkv_grad[:, local : 2 * local], qkv_grad[:, 2 * local :]], 1
    )
    return (
        result,
        grad_images,
        first_gain_g,
        first_shift_g,
        qkv_grad.astype(F32),
        own(query_g, local),
        own(value_g, local),
        output_grad.T.astype(F32),
        output_g,
        second_gain_g,
        second_shift_g,
        expand_grad.astype(F32),
        own(expand_g, hidden),
        shrink_grad.T.astype(F32),
        shrink_g,
    )


def solution(mesh):
    return jax.shard_map(
        functools.partial(shards, mesh.shape["tensor"]),
        mesh=mesh,
        in_specs=(
            P("dp", None, None),
            P(),
            P(),
            P(None, None, "tensor"),
            P("tensor"),
            P("tensor"),
            P("tensor", None),
            P(),
            P(),
            P(),
            P(None, "tensor"),
            P("tensor"),
            P("tensor", None),
            P(),
            P("dp", None, None),
        ),
        out_specs=(
            P("dp", None, None),
            P("dp", None, None),
            P(),
            P(),
            P(None, None, "tensor"),
            P("tensor"),
            P("tensor"),
            P("tensor", None),
            P(),
            P(),
            P(),
            P(None, "tensor"),
            P("tensor"),
            P("tensor", None),
            P(),
        ),
        check_vma=False,
    )
```
